32 devices in a mesh: ctx: 8 (over z, x), dp: 4 (over y, core).
Axes of the slice: x: 2, y: 2, z: 4, core: 2. Of those that a mesh axis runs over, the one named last changes fastest.
Arguments:
- query: bfloat16 [4, 2048, 1024], P('dp', 'ctx'), may hold values from -6 to 6
- keys: bfloat16 [4, 2048, 128], P('dp', 'ctx'), may hold values from -6 to 6
- values: bfloat16 [4, 2048, 128], P('dp', 'ctx'), may hold values from -6 to 6
- attn_out: bfloat16 [4, 2048, 1024], P('dp', 'ctx'), may hold values from -6 to 6
- out_grad: bfloat16 [4, 2048, 1024], P('dp', 'ctx'), may hold values from -6 to 6
- lse: float32 [4, 8, 2048], P('dp', None, 'ctx'), may hold values from 4 to 7
- doc_start: int32 [4, 2048], P('dp', 'ctx'), may hold values from 0 to 2047, as said below
- inputs: bfloat16 [4, 2048, 4096], P('dp', 'ctx'), may hold values from -6 to 6
Outputs:
- query_grad: bfloat16 [4, 2048, 1024], P('dp', 'ctx')
- key_grad: bfloat16 [4, 2048, 128], P('dp', 'ctx')
- value_grad: bfloat16 [4, 2048, 128], P('dp', 'ctx')
- key_weight_grad: float32 [4096, 128], P('dp')
The draws below stay inside these ranges and needn't reach their ends.
Inputs may be any that keep to these rules, and one draw needn't show every extreme that they name: doc_start[p, t] is the first position of the document that holds token t of pack p: it never falls along t, doc_start[p, t] <= t, it equals t exactly where a document begins, doc_start[p, 0] = 0, and the last position of every pack begins a document of its own; each pack holds the larger of 4 and 1 documents.
All inputs are finite; a program needn't handle non-finite values.
Results may differ from the reference program's by a relative error of at most 0.0055.
Values may be sent and summed in bfloat16 or wider, within the bound.
A program may use at most 64 MiB of HBM per device.

```python
import jax
import jax.numpy as jnp
from jax import lax

D = 4096
QH = 8
DH = 128
WINDOW = 256
TOK_DEV = 256
SEQ = 2048
PACKS = 4
N_CTX = 8


def draw_doc_start(key, part):
    key = jax.random.fold_in(key, 11)
    length = TOK_DEV * N_CTX
    docs = max(4, length // 2048)

    def one_pack(sub):
        inner = jax.random.permutation(sub, length - 2)[:docs - 2] + 1
        cuts = jnp.concatenate([inner.astype(jnp.int32), jnp.array([length - 1], jnp.int32)])
        marks = jnp.zeros((length,), jnp.int32).at[cuts].set(1)
        places = jnp.arange(length, dtype=jnp.int32) * marks
        return lax.cummax(places, axis=0)
    return jax.vmap(one_pack)(jax.random.split(key, PACKS))


def level_of(own_key, extent, pieces, least, top_value):
    level = 1.0
    for position, blocks in pieces:
        heights = jax.random.uniform(jax.random.fold_in(jax.random.fold_in(own_key, 6), position), (blocks,), jnp.float32, least / len(pieces), top_value / len(pieces))
        level = level * jnp.repeat(jnp.exp(heights), extent[position] // blocks).reshape((-1,) + (1,) * (len(extent) - 1 - position))
    return level


def scatter_about(key, extent, deviation, reach, pieces=(), kind=jnp.bfloat16):
    level = level_of(key, extent, pieces, -0.22, 0.18) if pieces else 1.0
    drawn = jax.random.normal(key, extent, jnp.float32) * deviation * level
    return jnp.minimum(jnp.maximum(drawn, -reach), reach).astype(kind)


def setup_inputs(seed: int = 0) -> dict:
    key_of = jax.random.split(jax.random.key(seed), 9)
    return {
        "query": scatter_about(key_of[0], (PACKS, SEQ, QH * DH), 1.0, 6.0, ((0, 4), (1, 8))),
        "keys": scatter_about(key_of[1], (PACKS, SEQ, DH), 1.0, 6.0, ((0, 4), (1, 8))),
        "values": scatter_about(key_of[2], (PACKS, SEQ, DH), 1.0, 6.0, ((0, 4), (1, 8))),
        "attn_out": scatter_about(key_of[3], (PACKS, SEQ, QH * DH), 1.0, 6.0, ((0, 4), (1, 8))),
        "out_grad": scatter_about(key_of[4], (PACKS, SEQ, QH * DH), 1.0, 6.0, ((0, 4), (1, 8))),
        "lse": jnp.clip(4.0 + 3.0 * jax.random.uniform(key_of[5], (PACKS, QH, SEQ), jnp.float32) ** level_of(key_of[5], (PACKS, QH, SEQ), ((0, 4), (2, 8)), -0.2, 0.2), 4.0, 7.0),
        "doc_start": draw_doc_start(jax.random.fold_in(key_of[8], 71), 0),
        "inputs": scatter_about(key_of[7], (PACKS, SEQ, D), 1.0, 6.0, ((0, 4), (1, 8))),
    }


def grad_block(query, dout, lse, delta, qpos, qstart, keys, values, kpos):
    rows = query.shape[0]
    q_three = query.astype(jnp.float32).reshape(rows, QH, DH)
    d_three = dout.astype(jnp.float32).reshape(rows, QH, DH)
    keys_f = keys.astype(jnp.float32)
    values_f = values.astype(jnp.float32)
    scale = DH ** -0.5
    scores = jnp.einsum("rhd,kd->hrk", q_three, keys_f)
    allowed = (kpos[None, :] >= qstart[:, None]) & (kpos[None, :] <= qpos[:, None]) & (qpos[:, None] - kpos[None, :] < WINDOW)
    probs = jnp.where(allowed[None], jnp.exp(scores * scale - lse[:, :, None]), 0.0)
    probs_low = probs.astype(jnp.bfloat16).astype(jnp.float32)
    value_part = jnp.einsum("hrk,rhd->kd", probs_low, d_three)
    dprob = jnp.einsum("rhd,kd->hrk", d_three, values_f)
    score_grad = (probs * (dprob - delta[:, :, None]) * scale).astype(jnp.bfloat16).astype(jnp.float32)
    query_part = jnp.einsum("hrk,kd->rhd", score_grad, keys_f).reshape(rows, QH * DH)
    key_part = jnp.einsum("hrk,rhd->kd", score_grad, q_three)
    return query_part, key_part, value_part


def pack_grads(items):
    query, keys, values, attn_out, out_grad, lse, doc_start, inputs = items
    seq = query.shape[0]
    nblk = seq // TOK_DEV
    rows = TOK_DEV
    delta = jnp.sum((out_grad.astype(jnp.float32) * attn_out.astype(jnp.float32)).reshape(seq, QH, DH), axis=-1).T
    places = jnp.arange(seq, dtype=jnp.int32)
    q_blk = query.reshape(nblk, rows, QH * DH)
    d_blk = out_grad.reshape(nblk, rows, QH * DH)
    k_blk = keys.reshape(nblk, rows, DH)
    v_blk = values.reshape(nblk, rows, DH)
    l_blk = lse.reshape(QH, nblk, rows).transpose(1, 0, 2)
    e_blk = delta.reshape(QH, nblk, rows).transpose(1, 0, 2)
    p_blk = places.reshape(nblk, rows)
    s_blk = doc_start.astype(jnp.int32).reshape(nblk, rows)

    def own(a):
        return grad_block(a[0], a[1], a[2], a[3], a[4], a[5], a[6], a[7], a[4])

    dq, dk, dv = lax.map(own, (q_blk, d_blk, l_blk, e_blk, p_blk, s_blk, k_blk, v_blk))
    tail = rows - WINDOW

    def cross(a):
        return grad_block(a[0], a[1], a[2], a[3], a[4], a[5], a[6], a[7], a[8])

    cq, ck, cv = lax.map(cross, (q_blk[1:, :WINDOW], d_blk[1:, :WINDOW], l_blk[1:, :, :WINDOW], e_blk[1:, :, :WINDOW], p_blk[1:, :WINDOW], s_blk[1:, :WINDOW], k_blk[:-1, tail:], v_blk[:-1, tail:], p_blk[:-1, tail:]))
    dq = dq.at[1:, :WINDOW].add(cq)
    dk = dk.at[:-1, tail:].add(ck)
    dv = dv.at[:-1, tail:].add(cv)
    dq_low = dq.reshape(seq, QH * DH).astype(jnp.bfloat16)
    dk_low = dk.reshape(seq, DH).astype(jnp.bfloat16)
    dv_low = dv.reshape(seq, DH).astype(jnp.bfloat16)
    term = lax.dot_general(inputs, dk_low, (((0,), (0,)), ((), ())), preferred_element_type=jnp.float32)
    return dq_low, dk_low, dv_low, term


def reference(query, keys, values, attn_out, out_grad, lse, doc_start, inputs):
    dq, dk, dv, terms = lax.map(pack_grads, (query, keys, values, attn_out, out_grad, lse, doc_start, inputs))
    return dq, dk, dv, jnp.sum(terms, axis=0)
```

```python
import functools

import jax
import jax.numpy as jnp
from jax import lax
from jax.experimental import pallas as pl
from jax.experimental.pallas import tpu as pltpu
from jax.sharding import PartitionSpec as P

QH = 8
WINDOW = 256
F32 = jnp.float32
BF16 = jnp.bfloat16
NT = (((1,), (1,)), ((), ()))


def dot(a, b):
    return jnp.dot(a, b, preferred_element_type=F32)


def dot_nt(a, b):
    return lax.dot_general(a, b, NT, preferred_element_type=F32)


def remote(src, dst, send, recv, where):
    return pltpu.make_async_remote_copy(
        src_ref=src, dst_ref=dst, send_sem=send, recv_sem=recv,
        device_id=where, device_id_type=pl.DeviceIdType.MESH,
    )


def kernel(n_ctx, n_dp, reduce_here, *refs):
    (q_in, k_in, v_in, o_in, g_in, lse_in, start_in, x_in) = refs[:8]
    n_out = 4 if reduce_here else 3
    outs = refs[8:8 + n_out]
    dq_out, dk_out, dv_out = outs[:3]
    scratch = refs[8 + n_out:]
    (q, k, v, o, g, lse, start, delta, kp, vp, ds_all, dq, dk_own, dv_own, dk_near, dv_near,
     dk_send, dv_send, dk_back, dv_back, dk_low, dv_low, load, store, halo_s, halo_r, back_s, back_r) = scratch[:28]
    rows, width = q.shape
    head = width // QH
    scale = head ** (-0.5)
    c = lax.axis_index("ctx")
    d = lax.axis_index("dp")
    after = lax.rem(c + 1, n_ctx)
    before = lax.rem(c + n_ctx - 1, n_ctx)

    loads = [
        pltpu.make_async_copy(src.at[0], dst, load.at[i])
        for i, (src, dst) in enumerate(
            ((k_in, k), (v_in, v), (q_in, q), (g_in, g), (o_in, o), (lse_in, lse))
        )
    ]
    loads.append(pltpu.make_async_copy(start_in, start, load.at[6]))
    for copy in loads:
        copy.start()

    partners = [(after, d), (before, d)]
    if reduce_here:
        (tot_out,) = outs[3:]
        (xl, xr, dkt, dkt_r, wf, s1, r1, s2, r2, s3, r3, gb, tot,
         xload, x_s, x_r, t_s, t_r, p1_s, p1_r, p2_s, p2_r, p3_s, p3_r, ag_s, ag_r) = scratch[28:]
        nz = n_ctx // 2
        block = x_in.shape[2] // n_dp
        core, y = lax.rem(d, 2), d // 2
        xx, z = lax.rem(c, 2), c // 2
        at_core = (c, y * 2 + 1 - core)
        at_y = (c, (1 - y) * 2 + core)
        at_x = (z * 2 + 1 - xx, d)
        at_z = [(lax.rem(z + s + 1, nz) * 2 + xx, d) for s in range(nz - 1)]
        partners += [at_core, at_y, at_x] + at_z
    barrier = pltpu.get_barrier_semaphore()
    for where in partners:
        pl.semaphore_signal(barrier, inc=1, device_id=where, device_id_type=pl.DeviceIdType.MESH)
    pl.semaphore_wait(barrier, len(partners))

    halo = [
        remote(src.at[0], dst, halo_s.at[i], halo_r.at[i], (after, d))
        for i, (src, dst) in enumerate(((k_in, kp), (v_in, vp)))
    ]
    for copy in halo:
        copy.start()
    if reduce_here:
        xcopies = []
        for yy in range(2):
            mine = pl.ds(pl.multiple_of((yy * 2 + core) * block, block), block)
            other = pl.ds(pl.multiple_of((yy * 2 + 1 - core) * block, block), block)
            xcopies.append(pltpu.make_async_copy(x_in.at[0, :, mine], xl.at[yy], xload.at[yy]))
            xcopies.append(remote(x_in.at[0, :, other], xr.at[yy], x_s.at[yy], x_r.at[yy], at_core))
        for copy in xcopies:
            copy.start()

    for copy in loads:
        copy.wait()
    lane = lax.broadcasted_iota(jnp.int32, (rows, 128), 1)
    spread = jnp.zeros((rows, 128), F32)
    for h in range(QH):
        cols = slice(h * head, (h + 1) * head)
        one = jnp.sum(g[:, cols].astype(F32) * o[:, cols].astype(F32), axis=1, keepdims=True)
        spread = jnp.where(lane == h, one, spread)
    delta[...] = spread.T[:QH]

    s_at = lax.broadcasted_iota(jnp.int32, (rows, rows), 0)
    t_at = lax.broadcasted_iota(jnp.int32, (rows, rows), 1)
    first = start[...] - c * rows

    def part(keys, values, allowed, base, dk_sum, dv_sum):
        def one(h):
            cols = pl.ds(pl.multiple_of(h * head, head), head)
            qh, gh = q[:, cols], g[:, cols]
            s = dot_nt(keys[...], qh)
            dp = dot_nt(values[...], gh)
            p = jnp.where(allowed, jnp.exp(s * scale - lse[pl.ds(h, 1), :]), 0.0)
            low = p.astype(BF16)
            sg = (p * (dp - delta[pl.ds(h, 1), :]) * scale).astype(BF16)
            ds_all[h, base:base + rows, :] = sg
            return dot(sg, qh), dot(low, gh)

        def body(i, carry):
            a, b = one(2 * i), one(2 * i + 1)
            dk_sum[...] += a[0] + b[0]
            dv_sum[...] += a[1] + b[1]
            return carry

        dk_sum[...] = jnp.zeros_like(dk_sum)
        dv_sum[...] = jnp.zeros_like(dv_sum)
        lax.fori_loop(0, QH // 2, body, 0)

    part(k, v, (s_at >= first) & (s_at <= t_at), 0, dk_own, dv_own)
    for copy in halo:
        copy.wait()
    part(kp, vp, (s_at - WINDOW >= first) & (t_at - s_at + WINDOW < WINDOW), rows, dk_near, dv_near)
    dk_send[...] = dk_near[...].astype(BF16)
    back = [
        remote(src, dst, back_s.at[i], back_r.at[i], (before, d))
        for i, (src, dst) in enumerate(((dk_send, dk_back), (dv_send, dv_back)))
    ]
    back[0].start()
    dv_send[...] = dv_near[...].astype(BF16)
    back[1].start()

    kt = jnp.concatenate([k[...].astype(F32).T, kp[...].astype(F32).T], axis=1).astype(BF16)

    def dq_body(i, carry):
        for h in (2 * i, 2 * i + 1):
            cols = pl.ds(pl.multiple_of(h * head, head), head)
            dq[:, cols] = dot(kt, ds_all[h]).T.astype(BF16)
        return carry

    lax.fori_loop(0, QH // 2, dq_body, 0)
    dq_store = pltpu.make_async_copy(dq, dq_out.at[0], store.at[0])
    dq_store.start()

    back[0].wait()
    dk = dk_own[...] + dk_back[...].astype(F32)
    dk_low[...] = dk.astype(BF16)
    dk_store = pltpu.make_async_copy(dk_low, dk_out.at[0], store.at[1])

    if reduce_here:
        dkt[...] = dk.T.astype(BF16)
        trade = remote(dkt, dkt_r, t_s.at[0], t_r.at[0], at_core)
        trade.start()
    dk_store.start()

    def finish_dv():
        back[1].wait()
        dv_low[...] = (dv_own[...] + dv_back[...].astype(F32)).astype(BF16)
        copy = pltpu.make_async_copy(dv_low, dv_out.at[0], store.at[2])
        copy.start()
        return copy

    if reduce_here:
        half = nz // 2
        for copy in xcopies:
            copy.wait()

        def pieces(yy, lo, hi, src, left, first_time):
            got = dot(left[...], src[yy, :, lo * 128:hi * 128])
            for j in range(lo, hi):
                piece = got[:, (j - lo) * 128:(j - lo + 1) * 128]
                if first_time:
                    wf[yy, j] = piece
                else:
                    wf[yy, j] += piece

        for yy in range(2):
            pieces(yy, 0, n_ctx, xl, dkt, True)
        trade.wait()
        for yy in range(2):
            pieces(yy, 0, n_ctx, xr, dkt_r, False)

        for j in range(n_ctx // 2):
            s1[0, j] = wf[1 - y, j].astype(BF16)
        e1 = [remote(s1.at[0], r1.at[0], p1_s.at[0], p1_r.at[0], at_y)]
        e1[0].start()
        for yy in range(2):
            for j in range(half):
                s1[1, yy * half + j] = wf[yy, (half + j) * 2 + 1 - xx].astype(BF16)
        e1.append(remote(s1.at[1], r1.at[1], p1_s.at[1], p1_r.at[1], at_x))
        e1[1].start()
        dv_store = finish_dv()

        e1[0].wait()
        for j in range(half):
            at = 2 * j + 1 - xx
            s2[0, j] = (wf[y, at] + r1[0, at].astype(F32)).astype(BF16)
        e2 = [remote(s2.at[0], r2.at[0], p2_s.at[0], p2_r.at[0], at_x)]
        e2[0].start()
        e1[1].wait()
        for j in range(half):
            at = (half + j) * 2 + xx
            s2[1, j] = (wf[1 - y, at] + r1[1, (1 - y) * half + j].astype(F32)).astype(BF16)
        e2.append(remote(s2.at[1], r2.at[1], p2_s.at[1], p2_r.at[1], at_y))
        e2[1].start()
        e2[0].wait()
        for j in range(half):
            at = 2 * j + xx
            s3[j] = wf[y, at] + r1[0, at].astype(F32) + r2[0, j].astype(F32)
        e2[1].wait()
        for j in range(half):
            at = (half + j) * 2 + xx
            s3[half + j] = wf[y, at] + r1[1, y * half + j].astype(F32) + r2[1, j].astype(F32)

        e3 = []
        for s in range(nz - 1):
            there = lax.rem(z + s + 1, nz)
            s1[0, s] = s3[there].astype(BF16)
            e3.append(remote(s1.at[0, s], r3.at[nz - 2 - s], p3_s.at[s], p3_r.at[nz - 2 - s], at_z[s]))
            e3[s].start()
        total = s3[z]
        for s in range(nz - 1):
            e3[s].wait_send()
        for s in range(nz - 1):
            e3[nz - 2 - s].wait_recv()
            total = total + r3[s].astype(F32)
        gb[c] = total.T.astype(BF16)

        sends = []
        over_z = [
            remote(gb.at[c], gb.at[c], ag_s.at[s], ag_r.at[s], at_z[s]) for s in range(nz - 1)
        ]
        own_x = remote(gb.at[c], gb.at[c], ag_s.at[nz - 1], ag_r.at[nz - 1], at_x)
        for copy in over_z:
            copy.start()
        own_x.start()
        passed = []
        for s in range(nz - 1):
            over_z[s].wait_recv()
            slot = lax.rem(z - s - 1 + nz, nz) * 2 + xx
            copy = remote(gb.at[slot], gb.at[slot], ag_s.at[nz + s], ag_r.at[nz + s], at_x)
            copy.start()
            passed.append(copy)
        own_x.wait_recv()
        for copy in passed:
            copy.wait_recv()
        tot[...] = gb[...].astype(F32).reshape(tot.shape)
        tot_store = pltpu.make_async_copy(tot, tot_out, store.at[3])
        tot_store.start()
        for copy in over_z + [own_x] + passed:
            copy.wait_send()
        tot_store.wait()
    else:
        dv_store = finish_dv()
    dq_store.wait()
    dk_store.wait()
    dv_store.wait()


def local(n_ctx, n_dp, query, keys, values, attn_out, out_grad, lse, doc_start, inputs):
    _, rows, width = query.shape
    head = width // QH
    depth = inputs.shape[2]
    reduce_here = n_dp == 4 and n_ctx % 4 == 0 and depth == n_dp * n_ctx * 128 and head == 128
    nz = n_ctx // 2
    any_space = pl.BlockSpec(memory_space=pl.ANY)
    out_shape = [
        jax.ShapeDtypeStruct(query.shape, BF16),
        jax.ShapeDtypeStruct(keys.shape, BF16),
        jax.ShapeDtypeStruct(keys.shape, BF16),
    ]
    dma = pltpu.SemaphoreType.DMA
    small = pltpu.VMEM((rows, head), BF16)
    wide = pltpu.VMEM((rows, head), F32)
    full = pltpu.VMEM((rows, width), BF16)
    scratch = [
        full, small, small, full, full, pltpu.VMEM((QH, rows), F32), pltpu.VMEM((1, rows), jnp.int32),
        pltpu.VMEM((QH, rows), F32), small, small, pltpu.VMEM((QH, 2 * rows, rows), BF16), full,
        wide, wide, wide, wide, small, small, small, small, small, small,
        dma((7,)), dma((4,)), dma((2,)), dma((2,)), dma((2,)), dma((2,)),
    ]
    if reduce_here:
        out_shape.append(jax.ShapeDtypeStruct((depth // n_dp, head), F32))
        scratch += [
            pltpu.VMEM((2, rows, depth // n_dp), BF16), pltpu.VMEM((2, rows, depth // n_dp), BF16),
            pltpu.VMEM((head, rows), BF16), pltpu.VMEM((head, rows), BF16),
            pltpu.VMEM((2, n_ctx, 128, 128), F32),
            pltpu.VMEM((2, nz, 128, 128), BF16), pltpu.VMEM((2, nz, 128, 128), BF16),
            pltpu.VMEM((2, nz // 2, 128, 128), BF16), pltpu.VMEM((2, nz // 2, 128, 128), BF16),
            pltpu.VMEM((nz, 128, 128), F32), pltpu.VMEM((nz - 1, 128, 128), BF16),
            pltpu.VMEM((n_ctx, 128, 128), BF16), pltpu.VMEM((depth // n_dp, head), F32),
            dma((2,)), dma((2,)), dma((2,)), dma((1,)), dma((1,)), dma((2,)), dma((2,)), dma((2,)), dma((2,)),
            dma((nz - 1,)), dma((nz - 1,)), dma((n_ctx - 1,)), dma((n_ctx - 1,)),
        ]
    got = pl.pallas_call(
        functools.partial(kernel, n_ctx, n_dp, reduce_here),
        out_shape=out_shape,
        in_specs=[any_space] * 8,
        out_specs=[any_space] * len(out_shape),
        scratch_shapes=scratch,
        compiler_params=pltpu.CompilerParams(
            collective_id=0, has_side_effects=True, vmem_limit_bytes=32 * 1024 * 1024
        ),
    )(query, keys, values, attn_out, out_grad, lse, doc_start, inputs)
    if reduce_here:
        return tuple(got)
    dq, dk, dv = got
    term = lax.dot_general(
        inputs[0], dk[0], (((0,), (0,)), ((), ())), preferred_element_type=jnp.float32
    )
    return dq, dk, dv, lax.psum(lax.psum_scatter(term, "dp", scatter_dimension=0, tiled=True), "ctx")


def solution(mesh):
    in_specs = (
        P("dp", "ctx", None),
        P("dp", "ctx", None),
        P("dp", "ctx", None),
        P("dp", "ctx", None),
        P("dp", "ctx", None),
        P("dp", None, "ctx"),
        P("dp", "ctx"),
        P("dp", "ctx", None),
    )
    out_specs = (P("dp", "ctx", None), P("dp", "ctx", None), P("dp", "ctx", None), P("dp", None))
    return jax.shard_map(
        functools.partial(local, mesh.shape["ctx"], mesh.shape["dp"]),
        mesh=mesh, in_specs=in_specs, out_specs=out_specs, check_vma=False,
    )
```

```python
import functools

import jax
import jax.numpy as jnp
from jax import lax
from jax.experimental import pallas as pl
from jax.experimental.pallas import tpu as pltpu
from jax.sharding import PartitionSpec as P

QH = 8
WINDOW = 256
F32 = jnp.float32
BF16 = jnp.bfloat16
NT = (((1,), (1,)), ((), ()))


def dot(a, b):
    return jnp.dot(a, b, preferred_element_type=F32)


def dot_nt(a, b):
    return lax.dot_general(a, b, NT, preferred_element_type=F32)


def remote(src, dst, send, recv, where):
    return pltpu.make_async_remote_copy(
        src_ref=src, dst_ref=dst, send_sem=send, recv_sem=recv,
        device_id=where, device_id_type=pl.DeviceIdType.MESH,
    )


def kernel(n_ctx, n_dp, reduce_here, *refs):
    (q_in, k_in, v_in, o_in, g_in, lse_in, start_in, x_in) = refs[:8]
    n_out = 4 if reduce_here else 3
    outs = refs[8:8 + n_out]
    dq_out, dk_out, dv_out = outs[:3]
    scratch = refs[8 + n_out:]
    (q, k, v, o, g, lse, start, delta, kp, vp, ds_all, dq, dk_own, dv_own, dk_near, dv_near,
     dk_send, dv_send, dk_back, dv_back, dk_low, dv_low, load, store, halo_s, halo_r, back_s, back_r) = scratch[:28]
    rows, width = q.shape
    head = width // QH
    scale = head ** (-0.5)
    c = lax.axis_index("ctx")
    d = lax.axis_index("dp")
    after = lax.rem(c + 1, n_ctx)
    before = lax.rem(c + n_ctx - 1, n_ctx)

    loads = [
        pltpu.make_async_copy(src.at[0], dst, load.at[i])
        for i, (src, dst) in enumerate(
            ((k_in, k), (v_in, v), (q_in, q), (g_in, g), (o_in, o), (lse_in, lse))
        )
    ]
    loads.append(pltpu.make_async_copy(start_in, start, load.at[6]))
    for copy in loads:
        copy.start()

    partners = [(after, d), (before, d)]
    if reduce_here:
        (tot_out,) = outs[3:]
        (xl, xr, dkt, dkt_r, wf, s1, r1, s2, r2, s3, r3, gb,
         xload, x_s, x_r, t_s, t_r, p1_s, p1_r, p2_s, p2_r, p3_s, p3_r, ag_s, ag_r) = scratch[28:]
        nz = n_ctx // 2
        block = x_in.shape[2] // n_dp
        core, y = lax.rem(d, 2), d // 2
        xx, z = lax.rem(c, 2), c // 2
        at_core = (c, y * 2 + 1 - core)
        at_y = (c, (1 - y) * 2 + core)
        at_x = (z * 2 + 1 - xx, d)
        at_z = [(lax.rem(z + s + 1, nz) * 2 + xx, d) for s in range(nz - 1)]
        partners += [at_core, at_y, at_x] + at_z
    barrier = pltpu.get_barrier_semaphore()
    for where in partners:
        pl.semaphore_signal(barrier, inc=1, device_id=where, device_id_type=pl.DeviceIdType.MESH)
    pl.semaphore_wait(barrier, len(partners))

    halo = [
        remote(src.at[0], dst, halo_s.at[i], halo_r.at[i], (after, d))
        for i, (src, dst) in enumerate(((k_in, kp), (v_in, vp)))
    ]
    for copy in halo:
        copy.start()
    for copy in loads:
        copy.wait()
    lane = lax.broadcasted_iota(jnp.int32, (rows, 128), 1)
    spread = jnp.zeros((rows, 128), F32)
    for h in range(QH):
        cols = slice(h * head, (h + 1) * head)
        one = jnp.sum(g[:, cols].astype(F32) * o[:, cols].astype(F32), axis=1, keepdims=True)
        spread = jnp.where(lane == h, one, spread)
    delta[...] = spread.T[:QH]

    s_at = lax.broadcasted_iota(jnp.int32, (rows, rows), 0)
    t_at = lax.broadcasted_iota(jnp.int32, (rows, rows), 1)
    first = start[...] - c * rows

    def part(keys, values, allowed, base, dk_sum, dv_sum):
        def one(h):
            cols = slice(h * head, (h + 1) * head)
            qh, gh = q[:, cols], g[:, cols]
            s = dot_nt(keys[...], qh)
            dp = dot_nt(values[...], gh)
            p = jnp.where(allowed, jnp.exp(s * scale - lse[h:h + 1, :]), 0.0)
            low = p.astype(BF16)
            sg = (p * (dp - delta[h:h + 1, :]) * scale).astype(BF16)
            ds_all[h, base:base + rows, :] = sg
            return dot(sg, qh), dot(low, gh)

        def body(i, carry):
            a, b = one(2 * i), one(2 * i + 1)
            dk_sum[...] += a[0] + b[0]
            dv_sum[...] += a[1] + b[1]
            return carry

        dk_sum[...] = jnp.zeros_like(dk_sum)
        dv_sum[...] = jnp.zeros_like(dv_sum)
        for i in range(QH // 2):
            body(i, 0)

    part(k, v, (s_at >= first) & (s_at <= t_at), 0, dk_own, dv_own)
    for copy in halo:
        copy.wait()
    if reduce_here:
        xcopies = []
        for yy in range(2):
            mine = pl.ds(pl.multiple_of((yy * 2 + core) * block, block), block)
            other = pl.ds(pl.multiple_of((yy * 2 + 1 - core) * block, block), block)
            xcopies.append(pltpu.make_async_copy(x_in.at[0, :, mine], xl.at[yy], xload.at[yy]))
            xcopies.append(remote(x_in.at[0, :, other], xr.at[yy], x_s.at[yy], x_r.at[yy], at_core))
        for copy in xcopies:
            copy.start()

    part(kp, vp, (s_at - WINDOW >= first) & (t_at - s_at + WINDOW < WINDOW), rows, dk_near, dv_near)
    dk_send[...] = dk_near[...].astype(BF16)
    back = [
        remote(src, dst, back_s.at[i], back_r.at[i], (before, d))
        for i, (src, dst) in enumerate(((dk_send, dk_back), (dv_send, dv_back)))
    ]
    back[0].start()
    dv_send[...] = dv_near[...].astype(BF16)
    back[1].start()

    kt = jnp.concatenate([k[...].astype(F32).T, kp[...].astype(F32).T], axis=1).astype(BF16)

    def dq_heads(lo, hi):
        for h in range(lo, hi):
            cols = slice(h * head, (h + 1) * head)
            dq[:, cols] = dot(kt, ds_all[h]).T.astype(BF16)

    def finish_dq():
        dq_heads(QH // 2, QH)
        copy = pltpu.make_async_copy(dq, dq_out.at[0], store.at[0])
        copy.start()
        return copy

    dq_heads(0, QH // 2)

    back[0].wait()
    dk = dk_own[...] + dk_back[...].astype(F32)
    dk_low[...] = dk.astype(BF16)
    dk_store = pltpu.make_async_copy(dk_low, dk_out.at[0], store.at[1])

    if reduce_here:
        dkt[...] = dk.T.astype(BF16)
        trade = remote(dkt, dkt_r, t_s.at[0], t_r.at[0], at_core)
        trade.start()
    dk_store.start()

    def finish_dv():
        back[1].wait()
        dv_low[...] = (dv_own[...] + dv_back[...].astype(F32)).astype(BF16)
        copy = pltpu.make_async_copy(dv_low, dv_out.at[0], store.at[2])
        copy.start()
        return copy

    if reduce_here:
        for copy in xcopies:
            copy.wait()
        order = []
        for j in range(nz // 2):
            order += [j, nz - 1 - j]
        away = 1 - y

        def chunk(src, left, yy, j):
            return dot(left[...], src[yy, :, j * 256:(j + 1) * 256])

        for yy in (away, y):
            for j in order:
                got = chunk(xl, dkt, yy, j)
                wf[yy, 2 * j] = got[:, :128]
                wf[yy, 2 * j + 1] = got[:, 128:]
        trade.wait()

        over_y, over_x = {}, {}
        for j in order:
            got = chunk(xr, dkt_r, away, j)
            s1[j, 0] = (wf[away, 2 * j] + got[:, :128]).astype(BF16)
            s1[j, 1] = (wf[away, 2 * j + 1] + got[:, 128:]).astype(BF16)
            over_y[j] = remote(s1.at[j], r1.at[j], p1_s.at[j], p1_r.at[j], at_y)
            over_y[j].start()
        for j in order:
            got = chunk(xr, dkt_r, y, j)
            wf[y, 2 * j] += got[:, :128]
            wf[y, 2 * j + 1] += got[:, 128:]

        def step_x(j):
            over_y[j].wait_recv()
            s2[j] = (wf[y, 2 * j + 1 - xx] + r1[j, 1 - xx].astype(F32)).astype(BF16)
            over_x[j] = remote(s2.at[j], r2.at[j], p2_s.at[j], p2_r.at[j], at_x)
            over_x[j].start()

        def to_owner(j):
            return remote(s3.at[j], r3.at[z], p3_s.at[j], p3_r.at[z], (j * 2 + xx, d))

        def step_z(j):
            over_x[j].wait_recv()
            kept = wf[y, 2 * j + xx] + r1[j, xx].astype(F32) + r2[j].astype(F32)
            wf[y, 2 * j + xx] = kept
            s3[j] = kept.astype(BF16)

            @pl.when(z != j)
            def _():
                to_owner(j).start()

        def over_z(t):
            return remote(gb.at[c], gb.at[c], ag_s.at[t], ag_r.at[z], (t * 2 + xx, d))

        def pass_x(j):
            at = j * 2 + xx
            return remote(gb.at[at], gb.at[at], ag_s.at[nz + j], ag_r.at[nz + j], at_x)

        def step_own(j):
            @pl.when(z == j)
            def _():
                total = wf[y, 2 * j + xx]
                for t in range(nz):
                    if t != j:
                        remote(s3.at[t], r3.at[t], p3_s.at[t], p3_r.at[t], at_y).wait_recv()
                        total = total + r3[t].astype(F32)
                gb[2 * j + xx] = total.T.astype(BF16)
                for t in range(nz):
                    if t != j:
                        over_z(t).start()
                pass_x(j).start()

        dv_store = finish_dv()
        dq_store = finish_dq()
        for i in range(nz + 2):
            if i < nz:
                step_x(order[i])
            if 1 <= i <= nz:
                step_z(order[i - 1])
            if i >= 2:
                step_own(order[i - 2])
        for j in order:
            @pl.when(z != j)
            def _():
                at = j * 2 + xx
                remote(gb.at[at], gb.at[at], ag_s.at[j], ag_r.at[j], at_y).wait_recv()
                pass_x(j).start()
        for j in order:
            at = j * 2 + 1 - xx
            remote(gb.at[at], gb.at[at], ag_s.at[nz + j], ag_r.at[nz + j], at_x).wait_recv()
        tot_store = pltpu.make_async_copy(gb, tot_out, store.at[3])
        tot_store.start()
        for j in order:
            over_y[j].wait_send()
            over_x[j].wait_send()
            pass_x(j).wait_send()

            @pl.when(z != j)
            def _():
                to_owner(j).wait_send()
                over_z(j).wait_send()
        tot_store.wait()
    else:
        dv_store = finish_dv()
        dq_store = finish_dq()
    dq_store.wait()
    dk_store.wait()
    dv_store.wait()


def hand_over_kernel(count, *refs):
    arrays, outs, held = refs[:count], refs[count:2 * count], refs[2 * count:3 * count]
    wide, arrive, leave = refs[3 * count:]
    loads = [pltpu.make_async_copy(arrays[i], held[i], arrive.at[i]) for i in range(count)]
    stores = [pltpu.make_async_copy(held[i], outs[i], leave.at[i]) for i in range(count - 1)]
    stores.append(pltpu.make_async_copy(wide, outs[-1], leave.at[count - 1]))
    places = [count - 1] + list(range(count - 1))
    for i in places:
        loads[i].start()
    for i in places:
        loads[i].wait()
        if i == count - 1:
            wide[...] = held[i][...].astype(F32).reshape(wide.shape)
        stores[i].start()
    for copy in stores:
        copy.wait()


def hand_over(arrays):
    *same, last = arrays
    count = len(arrays)
    total = jax.ShapeDtypeStruct((last.shape[0] * last.shape[1], last.shape[2]), F32)
    return pl.pallas_call(
        functools.partial(hand_over_kernel, count),
        out_shape=[jax.ShapeDtypeStruct(a.shape, a.dtype) for a in same] + [total],
        in_specs=[pl.BlockSpec(memory_space=pl.ANY)] * count,
        out_specs=[pl.BlockSpec(memory_space=pltpu.HBM)] * count,
        scratch_shapes=[pltpu.VMEM(a.shape, a.dtype) for a in arrays]
        + [pltpu.VMEM(total.shape, F32), pltpu.SemaphoreType.DMA((count,)), pltpu.SemaphoreType.DMA((count,))],
    )(*arrays)


def local(n_ctx, n_dp, query, keys, values, attn_out, out_grad, lse, doc_start, inputs):
    _, rows, width = query.shape
    head = width // QH
    depth = inputs.shape[2]
    reduce_here = n_dp == 4 and n_ctx % 4 == 0 and depth == n_dp * n_ctx * 128 and head == 128
    nz = n_ctx // 2
    any_space = pl.BlockSpec(memory_space=pl.ANY)
    out_shape = [
        jax.ShapeDtypeStruct(query.shape, BF16),
        jax.ShapeDtypeStruct(keys.shape, BF16),
        jax.ShapeDtypeStruct(keys.shape, BF16),
    ]
    dma = pltpu.SemaphoreType.DMA
    small = pltpu.VMEM((rows, head), BF16)
    wide = pltpu.VMEM((rows, head), F32)
    full = pltpu.VMEM((rows, width), BF16)
    scratch = [
        full, small, small, full, full, pltpu.VMEM((QH, rows), F32), pltpu.VMEM((1, rows), jnp.int32),
        pltpu.VMEM((QH, rows), F32), small, small, pltpu.VMEM((QH, 2 * rows, rows), BF16), full,
        wide, wide, wide, wide, small, small, small, small, small, small,
        dma((7,)), dma((4,)), dma((2,)), dma((2,)), dma((2,)), dma((2,)),
    ]
    if reduce_here:
        out_shape.append(jax.ShapeDtypeStruct((n_ctx, 128, head), BF16))
        scratch += [
            pltpu.VMEM((2, rows, depth // n_dp), BF16), pltpu.VMEM((2, rows, depth // n_dp), BF16),
            pltpu.VMEM((head, rows), BF16), pltpu.VMEM((head, rows), BF16),
            pltpu.VMEM((2, n_ctx, 128, 128), F32),
            pltpu.VMEM((nz, 2, 128, 128), BF16), pltpu.VMEM((nz, 2, 128, 128), BF16),
            pltpu.VMEM((nz, 128, 128), BF16), pltpu.VMEM((nz, 128, 128), BF16),
            pltpu.VMEM((nz, 128, 128), BF16), pltpu.VMEM((nz, 128, 128), BF16),
            pltpu.VMEM((n_ctx, 128, 128), BF16),
            dma((2,)), dma((2,)), dma((2,)), dma((1,)), dma((1,)), dma((nz,)), dma((nz,)), dma((nz,)), dma((nz,)),
            dma((nz,)), dma((nz,)), dma((2 * nz,)), dma((2 * nz,)),
        ]
    got = pl.pallas_call(
        functools.partial(kernel, n_ctx, n_dp, reduce_here),
        out_shape=out_shape,
        in_specs=[pl.BlockSpec(memory_space=pltpu.HBM)] * 8,
        out_specs=[any_space] * len(out_shape),
        scratch_shapes=scratch,
        compiler_params=pltpu.CompilerParams(
            collective_id=0, has_side_effects=True, vmem_limit_bytes=56 * 1024 * 1024
        ),
    )(query, keys, values, attn_out, out_grad, lse, doc_start, inputs)
    if reduce_here:
        return tuple(hand_over(got))
    dq, dk, dv = got
    term = lax.dot_general(
        inputs[0], dk[0], (((0,), (0,)), ((), ())), preferred_element_type=jnp.float32
    )
    return dq, dk, dv, lax.psum(lax.psum_scatter(term, "dp", scatter_dimension=0, tiled=True), "ctx")


def solution(mesh):
    in_specs = (
        P("dp", "ctx", None),
        P("dp", "ctx", None),
        P("dp", "ctx", None),
        P("dp", "ctx", None),
        P("dp", "ctx", None),
        P("dp", None, "ctx"),
        P("dp", "ctx"),
        P("dp", "ctx", None),
    )
    out_specs = (P("dp", "ctx", None), P("dp", "ctx", None), P("dp", "ctx", None), P("dp", None))
    return jax.shard_map(
        functools.partial(local, mesh.shape["ctx"], mesh.shape["dp"]),
        mesh=mesh, in_specs=in_specs, out_specs=out_specs, check_vma=False,
    )
```

```python
import functools

import jax
import jax.numpy as jnp
from jax import lax
from jax.experimental import pallas as pl
from jax.experimental.pallas import tpu as pltpu
from jax.sharding import PartitionSpec as P

QH = 8
WINDOW = 256
F32 = jnp.float32
BF16 = jnp.bfloat16
NT = (((1,), (1,)), ((), ()))


def dot(a, b):
    return jnp.dot(a, b, preferred_element_type=F32)


def dot_nt(a, b):
    return lax.dot_general(a, b, NT, preferred_element_type=F32)


def remote(src, dst, send, recv, where):
    return pltpu.make_async_remote_copy(
        src_ref=src, dst_ref=dst, send_sem=send, recv_sem=recv,
        device_id=where, device_id_type=pl.DeviceIdType.MESH,
    )


def kernel(n_ctx, n_dp, reduce_here, *refs):
    (q_in, k_in, v_in, o_in, g_in, lse_in, start_in, x_in) = refs[:8]
    n_out = 4 if reduce_here else 3
    outs = refs[8:8 + n_out]
    dq_out, dk_out, dv_out = outs[:3]
    scratch = refs[8 + n_out:]
    (q, k, v, o, g, lse, start, delta, kp, vp, ds_all, dq, dk_own, dv_own, dk_near, dv_near,
     dk_send, dv_send, dk_back, dv_back, dk_low, dv_low, load, store, halo_s, halo_r, back_s, back_r, probs) = scratch[:29]
    rows, width = q.shape
    head = width // QH
    scale = head ** (-0.5)
    c = lax.axis_index("ctx")
    d = lax.axis_index("dp")
    after = lax.rem(c + 1, n_ctx)
    before = lax.rem(c + n_ctx - 1, n_ctx)

    loads = [
        pltpu.make_async_copy(src.at[0], dst, load.at[i])
        for i, (src, dst) in enumerate(
            ((k_in, k), (v_in, v), (q_in, q), (g_in, g), (o_in, o), (lse_in, lse))
        )
    ]
    loads.append(pltpu.make_async_copy(start_in, start, load.at[6]))
    for copy in loads:
        copy.start()

    partners = [(after, d), (before, d)]
    if reduce_here:
        (tot_out,) = outs[3:]
        (xl, xr, dkt, dkt_r, wf, s1, r1, s2, r2, gb,
         xload, x_s, x_r, t_s, t_r, p1_s, p1_r, p2_s, p2_r, ag_s, ag_r) = scratch[29:]
        nz = n_ctx // 2
        block = x_in.shape[2] // n_dp
        core, y = lax.rem(d, 2), d // 2
        xx, z = lax.rem(c, 2), c // 2
        at_core = (c, y * 2 + 1 - core)
        at_y = (c, (1 - y) * 2 + core)
        far = [(s, e) for s in range(1, nz) for e in (0, 1)] + [(0, 1)]
        at = {(s, e): (lax.rem(z + s, nz) * 2 + (1 - xx if e else xx), d) for s, e in far}
        at_x = at[0, 1]
        partners += [at_core, at_y] + [at[one] for one in far]
    barrier = pltpu.get_barrier_semaphore()
    for where in partners:
        pl.semaphore_signal(barrier, inc=1, device_id=where, device_id_type=pl.DeviceIdType.MESH)
    pl.semaphore_wait(barrier, len(partners))

    halo = [
        remote(src.at[0], dst, halo_s.at[i], halo_r.at[i], (after, d))
        for i, (src, dst) in enumerate(((k_in, kp), (v_in, vp)))
    ]
    for copy in halo:
        copy.start()
    if reduce_here:
        xcopies = []
        for yy in range(2):
            mine = pl.ds(pl.multiple_of((yy * 2 + core) * block, block), block)
            other = pl.ds(pl.multiple_of((yy * 2 + 1 - core) * block, block), block)
            xcopies.append(pltpu.make_async_copy(x_in.at[0, :, mine], xl.at[yy], xload.at[yy]))
            xcopies.append(remote(x_in.at[0, :, other], xr.at[yy], x_s.at[yy], x_r.at[yy], at_core))
        for copy in xcopies:
            copy.start()

    for copy in loads:
        copy.wait()
    lane = lax.broadcasted_iota(jnp.int32, (rows, 128), 1)
    spread = jnp.zeros((rows, 128), F32)
    for h in range(QH):
        cols = slice(h * head, (h + 1) * head)
        one = jnp.sum(g[:, cols].astype(F32) * o[:, cols].astype(F32), axis=1, keepdims=True)
        spread = jnp.where(lane == h, one, spread)
    delta[...] = spread.T[:QH]

    s_at = lax.broadcasted_iota(jnp.int32, (rows, rows), 0)
    t_at = lax.broadcasted_iota(jnp.int32, (rows, rows), 1)
    first = start[...] - c * rows

    def part(keys, values, allowed, base, dk_sum, dv_sum):
        def one(h):
            cols = slice(h * head, (h + 1) * head)
            qh, gh = q[:, cols], g[:, cols]
            s = dot_nt(keys[...], qh)
            dp = dot_nt(values[...], gh)
            p = jnp.where(allowed, jnp.exp(s * scale - lse[h:h + 1, :]), 0.0)
            low = p.astype(BF16)
            sg = (p * (dp - delta[h:h + 1, :]) * scale).astype(BF16)
            ds_all[h, base:base + rows, :] = sg
            return dot(sg, qh), dot(low, gh)

        def body(i, carry):
            a, b = one(2 * i), one(2 * i + 1)
            dk_sum[...] += a[0] + b[0]
            dv_sum[...] += a[1] + b[1]
            return carry

        dk_sum[...] = jnp.zeros_like(dk_sum)
        dv_sum[...] = jnp.zeros_like(dv_sum)
        for i in range(QH // 2):
            body(i, 0)

    part(k, v, (s_at >= first) & (s_at <= t_at), 0, dk_own, dv_own)
    near = (s_at - WINDOW >= first) & (t_at - s_at + WINDOW < WINDOW)
    halo[0].wait()
    for h in range(QH):
        cols = slice(h * head, (h + 1) * head)
        score = dot_nt(kp[...], q[:, cols]) * scale - lse[h:h + 1, :]
        p = jnp.where(near, jnp.exp(score), 0.0)
        probs[h] = p
        term = dot(p.astype(BF16), g[:, cols])
        dv_near[...] = term if h == 0 else dv_near[...] + term
    halo[1].wait()
    for h in range(QH):
        cols = slice(h * head, (h + 1) * head)
        dp = dot_nt(vp[...], g[:, cols])
        sg = (probs[h] * (dp - delta[h:h + 1, :]) * scale).astype(BF16)
        ds_all[h, rows:, :] = sg
        term = dot(sg, q[:, cols])
        dk_near[...] = term if h == 0 else dk_near[...] + term
    dk_send[...] = dk_near[...].astype(BF16)
    back = [
        remote(src, dst, back_s.at[i], back_r.at[i], (before, d))
        for i, (src, dst) in enumerate(((dk_send, dk_back), (dv_send, dv_back)))
    ]
    back[0].start()
    dv_send[...] = dv_near[...].astype(BF16)
    back[1].start()

    kt = jnp.concatenate([k[...].astype(F32).T, kp[...].astype(F32).T], axis=1).astype(BF16)

    def dq_heads(lo, hi):
        for h in range(lo, hi):
            cols = slice(h * head, (h + 1) * head)
            dq[:, cols] = dot(kt, ds_all[h]).T.astype(BF16)

    def finish_dq():
        dq_heads(QH // 2, QH)
        copy = pltpu.make_async_copy(dq, dq_out.at[0], store.at[0])
        copy.start()
        return copy

    dq_heads(0, QH // 2)

    back[0].wait()
    dk = dk_own[...] + dk_back[...].astype(F32)
    dk_low[...] = dk.astype(BF16)
    dk_store = pltpu.make_async_copy(dk_low, dk_out.at[0], store.at[1])

    if reduce_here:
        dkt[...] = dk.T.astype(BF16)
        trade = remote(dkt, dkt_r, t_s.at[0], t_r.at[0], at_core)
        trade.start()
    dk_store.start()

    def finish_dv():
        back[1].wait()
        dv_low[...] = (dv_own[...] + dv_back[...].astype(F32)).astype(BF16)
        copy = pltpu.make_async_copy(dv_low, dv_out.at[0], store.at[2])
        copy.start()
        return copy

    if reduce_here:
        for copy in xcopies:
            copy.wait()
        steps = list(range(1, nz)) + [0]
        places = [lax.rem(z + s, nz) for s in range(nz)]

        def chunk(src, left, yy, s):
            cols = pl.ds(pl.multiple_of(places[s] * 256, 256), 256)
            return dot(left[...], src[yy, :, cols])

        for yy in (1 - y, y):
            for s in steps:
                got = chunk(xl, dkt, yy, s)
                wf[yy, 2 * s] = got[:, :128]
                wf[yy, 2 * s + 1] = got[:, 128:]
        trade.wait()

        over_y = {}
        for s in steps:
            got = chunk(xr, dkt_r, 1 - y, s)
            s1[s, 0] = (wf[1 - y, 2 * s] + got[:, :128]).astype(BF16)
            s1[s, 1] = (wf[1 - y, 2 * s + 1] + got[:, 128:]).astype(BF16)
            over_y[s] = remote(s1.at[s], r1.at[s], p1_s.at[s], p1_r.at[s], at_y)
            over_y[s].start()
        for s in steps:
            got = chunk(xr, dkt_r, y, s)
            wf[y, 2 * s] += got[:, :128]
            wf[y, 2 * s + 1] += got[:, 128:]
        dv_store = finish_dv()
        dq_store = finish_dq()

        out = {}
        for s in steps:
            over_y[s].wait_recv()
            for e in (0, 1):
                half = 1 - xx if e else xx
                piece = wf[y, 2 * s + half] + r1[s, half].astype(F32)
                if (s, e) == (0, 0):
                    total = piece
                    continue
                n = 2 * s + e
                s2[n] = piece.astype(BF16)
                out[s, e] = remote(s2.at[n], r2.at[n], p2_s.at[n], p2_r.at[n], at[s, e])
                out[s, e].start()
        for s, e in far:
            out[s, e].wait_recv()
            total = total + r2[2 * s + e].astype(F32)
        gb[c] = total.T.astype(BF16)

        over_z = [
            remote(gb.at[c], gb.at[c], ag_s.at[s], ag_r.at[s], at[s, 0]) for s in range(1, nz)
        ]
        over_x = [remote(gb.at[c], gb.at[c], ag_s.at[nz], ag_r.at[nz], at_x)]
        for copy in over_z + over_x:
            copy.start()
        for s in range(1, nz):
            over_z[s - 1].wait_recv()
            slot = lax.rem(z - s + nz, nz) * 2 + xx
            copy = remote(gb.at[slot], gb.at[slot], ag_s.at[nz + s], ag_r.at[nz + s], at_x)
            copy.start()
            over_x.append(copy)
        for copy in over_x:
            copy.wait_recv()
        tot_store = pltpu.make_async_copy(gb, tot_out, store.at[3])
        tot_store.start()
        for copy in list(over_y.values()) + list(out.values()) + over_z + over_x:
            copy.wait_send()
        tot_store.wait()
    else:
        dv_store = finish_dv()
        dq_store = finish_dq()
    dq_store.wait()
    dk_store.wait()
    dv_store.wait()


def hand_over_kernel(count, *refs):
    arrays, outs, held = refs[:count], refs[count:2 * count], refs[2 * count:3 * count]
    wide, arrive, leave = refs[3 * count:]
    loads = [pltpu.make_async_copy(arrays[i], held[i], arrive.at[i]) for i in range(count)]
    stores = [pltpu.make_async_copy(held[i], outs[i], leave.at[i]) for i in range(count - 1)]
    stores.append(pltpu.make_async_copy(wide, outs[-1], leave.at[count - 1]))
    places = [count - 1] + list(range(count - 1))
    for i in places:
        loads[i].start()
    for i in places:
        loads[i].wait()
        if i == count - 1:
            wide[...] = held[i][...].astype(F32).reshape(wide.shape)
        stores[i].start()
    for copy in stores:
        copy.wait()


def hand_over(arrays):
    *same, last = arrays
    count = len(arrays)
    total = jax.ShapeDtypeStruct((last.shape[0] * last.shape[1], last.shape[2]), F32)
    return pl.pallas_call(
        functools.partial(hand_over_kernel, count),
        out_shape=[jax.ShapeDtypeStruct(a.shape, a.dtype) for a in same] + [total],
        in_specs=[pl.BlockSpec(memory_space=pl.ANY)] * count,
        out_specs=[pl.BlockSpec(memory_space=pltpu.HBM)] * count,
        scratch_shapes=[pltpu.VMEM(a.shape, a.dtype) for a in arrays]
        + [pltpu.VMEM(total.shape, F32), pltpu.SemaphoreType.DMA((count,)), pltpu.SemaphoreType.DMA((count,))],
    )(*arrays)


def local(n_ctx, n_dp, query, keys, values, attn_out, out_grad, lse, doc_start, inputs):
    _, rows, width = query.shape
    head = width // QH
    depth = inputs.shape[2]
    reduce_here = n_dp == 4 and n_ctx % 4 == 0 and depth == n_dp * n_ctx * 128 and head == 128
    nz = n_ctx // 2
    any_space = pl.BlockSpec(memory_space=pl.ANY)
    out_shape = [
        jax.ShapeDtypeStruct(query.shape, BF16),
        jax.ShapeDtypeStruct(keys.shape, BF16),
        jax.ShapeDtypeStruct(keys.shape, BF16),
    ]
    dma = pltpu.SemaphoreType.DMA
    small = pltpu.VMEM((rows, head), BF16)
    wide = pltpu.VMEM((rows, head), F32)
    full = pltpu.VMEM((rows, width), BF16)
    scratch = [
        full, small, small, full, full, pltpu.VMEM((QH, rows), F32), pltpu.VMEM((1, rows), jnp.int32),
        pltpu.VMEM((QH, rows), F32), small, small, pltpu.VMEM((QH, 2 * rows, rows), BF16), full,
        wide, wide, wide, wide, small, small, small, small, small, small,
        dma((7,)), dma((4,)), dma((2,)), dma((2,)), dma((2,)), dma((2,)),
        pltpu.VMEM((QH, rows, rows), F32),
    ]
    if reduce_here:
        out_shape.append(jax.ShapeDtypeStruct((n_ctx, 128, head), BF16))
        scratch += [
            pltpu.VMEM((2, rows, depth // n_dp), BF16), pltpu.VMEM((2, rows, depth // n_dp), BF16),
            pltpu.VMEM((head, rows), BF16), pltpu.VMEM((head, rows), BF16),
            pltpu.VMEM((2, n_ctx, 128, 128), F32),
            pltpu.VMEM((nz, 2, 128, 128), BF16), pltpu.VMEM((nz, 2, 128, 128), BF16),
            pltpu.VMEM((n_ctx, 128, 128), BF16), pltpu.VMEM((n_ctx, 128, 128), BF16),
            pltpu.VMEM((n_ctx, 128, 128), BF16),
            dma((2,)), dma((2,)), dma((2,)), dma((1,)), dma((1,)), dma((nz,)), dma((nz,)), dma((n_ctx,)), dma((n_ctx,)),
            dma((2 * nz,)), dma((2 * nz,)),
        ]
    got = pl.pallas_call(
        functools.partial(kernel, n_ctx, n_dp, reduce_here),
        out_shape=out_shape,
        in_specs=[pl.BlockSpec(memory_space=pltpu.HBM)] * 8,
        out_specs=[any_space] * len(out_shape),
        scratch_shapes=scratch,
        compiler_params=pltpu.CompilerParams(
            collective_id=0, has_side_effects=True, vmem_limit_bytes=56 * 1024 * 1024
        ),
    )(query, keys, values, attn_out, out_grad, lse, doc_start, inputs)
    if reduce_here:
        return tuple(hand_over(got))
    dq, dk, dv = got
    term = lax.dot_general(
        inputs[0], dk[0], (((0,), (0,)), ((), ())), preferred_element_type=jnp.float32
    )
    return dq, dk, dv, lax.psum(lax.psum_scatter(term, "dp", scatter_dimension=0, tiled=True), "ctx")


def solution(mesh):
    in_specs = (
        P("dp", "ctx", None),
        P("dp", "ctx", None),
        P("dp", "ctx", None),
        P("dp", "ctx", None),
        P("dp", "ctx", None),
        P("dp", None, "ctx"),
        P("dp", "ctx"),
        P("dp", "ctx", None),
    )
    out_specs = (P("dp", "ctx", None), P("dp", "ctx", None), P("dp", "ctx", None), P("dp", None))
    return jax.shard_map(
        functools.partial(local, mesh.shape["ctx"], mesh.shape["dp"]),
        mesh=mesh, in_specs=in_specs, out_specs=out_specs, check_vma=False,
    )
```

```python
import functools

import jax
import jax.numpy as jnp
from jax import lax
from jax.experimental import pallas as pl
from jax.experimental.pallas import tpu as pltpu
from jax.sharding import PartitionSpec as P

QH = 8
WINDOW = 256
F32 = jnp.float32
BF16 = jnp.bfloat16
NT = (((1,), (1,)), ((), ()))


def dot(a, b):
    return jnp.dot(a, b, preferred_element_type=F32)


def dot_nt(a, b):
    return lax.dot_general(a, b, NT, preferred_element_type=F32)


def remote(src, dst, send, recv, where):
    return pltpu.make_async_remote_copy(
        src_ref=src, dst_ref=dst, send_sem=send, recv_sem=recv,
        device_id=where, device_id_type=pl.DeviceIdType.MESH,
    )


def kernel(n_ctx, n_dp, reduce_here, *refs):
    (q_in, k_in, v_in, o_in, g_in, lse_in, start_in, x_in) = refs[:8]
    n_out = 4 if reduce_here else 3
    outs = refs[8:8 + n_out]
    dq_out, dk_out, dv_out = outs[:3]
    scratch = refs[8 + n_out:]
    (q, k, v, o, g, lse, start, delta, kp, vp, ds_all, dq, dk_own, dv_own, dk_near, dv_near,
     dk_send, dv_send, dk_back, dv_back, dk_low, dv_low, load, store, halo_s, halo_r, back_s, back_r, probs) = scratch[:29]
    rows, width = q.shape
    head = width // QH
    scale = head ** (-0.5)
    c = lax.axis_index("ctx")
    d = lax.axis_index("dp")
    after = lax.rem(c + 1, n_ctx)
    before = lax.rem(c + n_ctx - 1, n_ctx)

    loads = [
        pltpu.make_async_copy(src.at[0], dst, load.at[i])
        for i, (src, dst) in enumerate(
            ((k_in, k), (v_in, v), (q_in, q), (g_in, g), (o_in, o), (lse_in, lse))
        )
    ]
    loads.append(pltpu.make_async_copy(start_in, start, load.at[6]))
    for copy in loads:
        copy.start()

    partners = [(after, d), (before, d)]
    if reduce_here:
        (tot_out,) = outs[3:]
        (xl, xr, dkt, dkt_r, wf, s1, r1, s2, r2, s3, r3, gb,
         xload, x_s, x_r, t_s, t_r, p1_s, p1_r, p2_s, p2_r, p3_s, p3_r, ag_s, ag_r) = scratch[29:]
        nz = n_ctx // 2
        block = x_in.shape[2] // n_dp
        core, y = lax.rem(d, 2), d // 2
        xx, z = lax.rem(c, 2), c // 2
        at_core = (c, y * 2 + 1 - core)
        at_y = (c, (1 - y) * 2 + core)
        far = [(s, e) for s in range(1, nz) for e in (0, 1)] + [(0, 1)]
        at = {(s, e): (lax.rem(z + s, nz) * 2 + (1 - xx if e else xx), d) for s, e in far}
        at_x = at[0, 1]
        partners += [at_core, at_y] + [at[one] for one in far]
    barrier = pltpu.get_barrier_semaphore()
    for where in partners:
        pl.semaphore_signal(barrier, inc=1, device_id=where, device_id_type=pl.DeviceIdType.MESH)
    pl.semaphore_wait(barrier, len(partners))

    halo = [
        remote(src.at[0], dst, halo_s.at[i], halo_r.at[i], (after, d))
        for i, (src, dst) in enumerate(((k_in, kp), (v_in, vp)))
    ]
    for copy in halo:
        copy.start()
    if reduce_here:
        xcopies = []
        for yy in range(2):
            mine = pl.ds(pl.multiple_of((yy * 2 + core) * block, block), block)
            other = pl.ds(pl.multiple_of((yy * 2 + 1 - core) * block, block), block)
            xcopies.append(pltpu.make_async_copy(x_in.at[0, :, mine], xl.at[yy], xload.at[yy]))
            xcopies.append(remote(x_in.at[0, :, other], xr.at[yy], x_s.at[yy], x_r.at[yy], at_core))
        for copy in xcopies:
            copy.start()

    for copy in loads:
        copy.wait()
    lane = lax.broadcasted_iota(jnp.int32, (rows, 128), 1)
    spread = jnp.zeros((rows, 128), F32)
    for h in range(QH):
        cols = slice(h * head, (h + 1) * head)
        one = jnp.sum(g[:, cols].astype(F32) * o[:, cols].astype(F32), axis=1, keepdims=True)
        spread = jnp.where(lane == h, one, spread)
    delta[...] = spread.T[:QH]

    s_at = lax.broadcasted_iota(jnp.int32, (rows, rows), 0)
    t_at = lax.broadcasted_iota(jnp.int32, (rows, rows), 1)
    first = start[...] - c * rows

    def part(keys, values, allowed, base, dk_sum, dv_sum):
        def one(h):
            cols = slice(h * head, (h + 1) * head)
            qh, gh = q[:, cols], g[:, cols]
            s = dot_nt(keys[...], qh)
            dp = dot_nt(values[...], gh)
            p = jnp.where(allowed, jnp.exp(s * scale - lse[h:h + 1, :]), 0.0)
            low = p.astype(BF16)
            sg = (p * (dp - delta[h:h + 1, :]) * scale).astype(BF16)
            ds_all[h, base:base + rows, :] = sg
            return dot(sg, qh), dot(low, gh)

        def body(i, carry):
            a, b = one(2 * i), one(2 * i + 1)
            dk_sum[...] += a[0] + b[0]
            dv_sum[...] += a[1] + b[1]
            return carry

        dk_sum[...] = jnp.zeros_like(dk_sum)
        dv_sum[...] = jnp.zeros_like(dv_sum)
        for i in range(QH // 2):
            body(i, 0)

    part(k, v, (s_at >= first) & (s_at <= t_at), 0, dk_own, dv_own)
    near = (s_at - WINDOW >= first) & (t_at - s_at + WINDOW < WINDOW)
    halo[0].wait()
    for h in range(QH):
        cols = slice(h * head, (h + 1) * head)
        score = dot_nt(kp[...], q[:, cols]) * scale - lse[h:h + 1, :]
        p = jnp.where(near, jnp.exp(score), 0.0)
        probs[h] = p
        term = dot(p.astype(BF16), g[:, cols])
        dv_near[...] = term if h == 0 else dv_near[...] + term
    halo[1].wait()
    for h in range(QH):
        cols = slice(h * head, (h + 1) * head)
        dp = dot_nt(vp[...], g[:, cols])
        sg = (probs[h] * (dp - delta[h:h + 1, :]) * scale).astype(BF16)
        ds_all[h, rows:, :] = sg
        term = dot(sg, q[:, cols])
        dk_near[...] = term if h == 0 else dk_near[...] + term
    dk_send[...] = dk_near[...].astype(BF16)
    back = [
        remote(src, dst, back_s.at[i], back_r.at[i], (before, d))
        for i, (src, dst) in enumerate(((dk_send, dk_back), (dv_send, dv_back)))
    ]
    back[0].start()
    dv_send[...] = dv_near[...].astype(BF16)
    back[1].start()

    kt = jnp.concatenate([k[...].astype(F32).T, kp[...].astype(F32).T], axis=1).astype(BF16)

    def dq_heads(lo, hi):
        for h in range(lo, hi):
            cols = slice(h * head, (h + 1) * head)
            dq[:, cols] = dot(kt, ds_all[h]).T.astype(BF16)

    def finish_dq():
        dq_heads(QH // 2, QH)
        copy = pltpu.make_async_copy(dq, dq_out.at[0], store.at[0])
        copy.start()
        return copy

    dq_heads(0, QH // 2)

    back[0].wait()
    dk = dk_own[...] + dk_back[...].astype(F32)
    dk_low[...] = dk.astype(BF16)
    dk_store = pltpu.make_async_copy(dk_low, dk_out.at[0], store.at[1])

    if reduce_here:
        dkt[...] = dk.T.astype(BF16)
        trade = remote(dkt, dkt_r, t_s.at[0], t_r.at[0], at_core)
        trade.start()
    dk_store.start()

    def finish_dv():
        back[1].wait()
        dv_low[...] = (dv_own[...] + dv_back[...].astype(F32)).astype(BF16)
        copy = pltpu.make_async_copy(dv_low, dv_out.at[0], store.at[2])
        copy.start()
        return copy

    if reduce_here:
        for copy in xcopies:
            copy.wait()
        steps = list(range(1, nz)) + [0]
        places = [lax.rem(z + s, nz) for s in range(nz)]

        def chunk(src, left, yy, s):
            cols = pl.ds(pl.multiple_of(places[s] * 256, 256), 256)
            return dot(left[...], src[yy, :, cols])

        for yy in (1 - y, y):
            for s in steps:
                got = chunk(xl, dkt, yy, s)
                wf[yy, 2 * s] = got[:, :128]
                wf[yy, 2 * s + 1] = got[:, 128:]
        trade.wait()

        def add(yy, s):
            got = chunk(xr, dkt_r, yy, s)
            wf[yy, 2 * s] += got[:, :128]
            wf[yy, 2 * s + 1] += got[:, 128:]

        first_out, second_out, out = {}, {}, {}
        for s in steps:
            add(1 - y, s)
            if s % 2:
                s1[s, 0] = wf[1 - y, 2 * s].astype(BF16)
                s1[s, 1] = wf[1 - y, 2 * s + 1].astype(BF16)
            else:
                add(y, s)
                s1[s, 0] = wf[0, 2 * s + 1 - xx].astype(BF16)
                s1[s, 1] = wf[1, 2 * s + 1 - xx].astype(BF16)
            first_out[s] = remote(
                s1.at[s], r1.at[s], p1_s.at[s], p1_r.at[s], at_y if s % 2 else at_x
            )
            first_out[s].start()
        for s in steps:
            if s % 2:
                add(y, s)

        def to_owner(s, e, piece):
            n = 2 * s + e
            s2[n] = piece.astype(BF16)
            out[s, e] = remote(s2.at[n], r2.at[n], p2_s.at[n], p2_r.at[n], at[s, e])
            out[s, e].start()

        for s in steps:
            first_out[s].wait_recv()
            if s % 2:
                for e in (0, 1):
                    half = 1 - xx if e else xx
                    to_owner(s, e, wf[y, 2 * s + half] + r1[s, half].astype(F32))
            else:
                s3[s] = (wf[1 - y, 2 * s + xx] + r1[s, 1 - y].astype(F32)).astype(BF16)
                second_out[s] = remote(s3.at[s], r3.at[s], p3_s.at[s], p3_r.at[s], at_y)
                second_out[s].start()
        for s in steps:
            if s % 2 == 0:
                second_out[s].wait_recv()
                piece = wf[y, 2 * s + xx] + r1[s, y].astype(F32) + r3[s].astype(F32)
                if s:
                    to_owner(s, 0, piece)
                else:
                    total = piece
        dv_store = finish_dv()
        dq_store = finish_dq()
        for s, e in out:
            out[s, e].wait_recv()
            total = total + r2[2 * s + e].astype(F32)
        gb[c] = total.T.astype(BF16)

        over_z = [
            remote(gb.at[c], gb.at[c], ag_s.at[s], ag_r.at[s], at[s, 0]) for s in range(1, nz)
        ]
        over_x = [remote(gb.at[c], gb.at[c], ag_s.at[nz], ag_r.at[nz], at_x)]
        for copy in over_z + over_x:
            copy.start()
        for s in range(1, nz):
            over_z[s - 1].wait_recv()
            slot = lax.rem(z - s + nz, nz) * 2 + xx
            copy = remote(gb.at[slot], gb.at[slot], ag_s.at[nz + s], ag_r.at[nz + s], at_x)
            copy.start()
            over_x.append(copy)
        for copy in over_x:
            copy.wait_recv()
        tot_store = pltpu.make_async_copy(gb, tot_out, store.at[3])
        tot_store.start()
        for copy in [*first_out.values(), *second_out.values(), *out.values()] + over_z + over_x:
            copy.wait_send()
        tot_store.wait()
    else:
        dv_store = finish_dv()
        dq_store = finish_dq()
    dq_store.wait()
    dk_store.wait()
    dv_store.wait()


def hand_over_kernel(count, *refs):
    arrays, outs, held = refs[:count], refs[count:2 * count], refs[2 * count:3 * count]
    wide, arrive, leave = refs[3 * count:]
    loads = [pltpu.make_async_copy(arrays[i], held[i], arrive.at[i]) for i in range(count)]
    stores = [pltpu.make_async_copy(held[i], outs[i], leave.at[i]) for i in range(count - 1)]
    stores.append(pltpu.make_async_copy(wide, outs[-1], leave.at[count - 1]))
    places = [count - 1] + list(range(count - 1))
    for i in places:
        loads[i].start()
    for i in places:
        loads[i].wait()
        if i == count - 1:
            wide[...] = held[i][...].astype(F32).reshape(wide.shape)
        stores[i].start()
    for copy in stores:
        copy.wait()


def hand_over(arrays):
    *same, last = arrays
    count = len(arrays)
    total = jax.ShapeDtypeStruct((last.shape[0] * last.shape[1], last.shape[2]), F32)
    return pl.pallas_call(
        functools.partial(hand_over_kernel, count),
        out_shape=[jax.ShapeDtypeStruct(a.shape, a.dtype) for a in same] + [total],
        in_specs=[pl.BlockSpec(memory_space=pl.ANY)] * count,
        out_specs=[pl.BlockSpec(memory_space=pltpu.HBM)] * count,
        scratch_shapes=[pltpu.VMEM(a.shape, a.dtype) for a in arrays]
        + [pltpu.VMEM(total.shape, F32), pltpu.SemaphoreType.DMA((count,)), pltpu.SemaphoreType.DMA((count,))],
    )(*arrays)


def local(n_ctx, n_dp, query, keys, values, attn_out, out_grad, lse, doc_start, inputs):
    _, rows, width = query.shape
    head = width // QH
    depth = inputs.shape[2]
    reduce_here = n_dp == 4 and n_ctx % 4 == 0 and rows == WINDOW and depth == n_dp * n_ctx * 128 and head == 128
    nz = n_ctx // 2
    any_space = pl.BlockSpec(memory_space=pl.ANY)
    out_shape = [
        jax.ShapeDtypeStruct(query.shape, BF16),
        jax.ShapeDtypeStruct(keys.shape, BF16),
        jax.ShapeDtypeStruct(keys.shape, BF16),
    ]
    dma = pltpu.SemaphoreType.DMA
    small = pltpu.VMEM((rows, head), BF16)
    wide = pltpu.VMEM((rows, head), F32)
    full = pltpu.VMEM((rows, width), BF16)
    scratch = [
        full, small, small, full, full, pltpu.VMEM((QH, rows), F32), pltpu.VMEM((1, rows), jnp.int32),
        pltpu.VMEM((QH, rows), F32), small, small, pltpu.VMEM((QH, 2 * rows, rows), BF16), full,
        wide, wide, wide, wide, small, small, small, small, small, small,
        dma((7,)), dma((4,)), dma((2,)), dma((2,)), dma((2,)), dma((2,)),
        pltpu.VMEM((QH, rows, rows), F32),
    ]
    if reduce_here:
        out_shape.append(jax.ShapeDtypeStruct((n_ctx, 128, head), BF16))
        scratch += [
            pltpu.VMEM((2, rows, depth // n_dp), BF16), pltpu.VMEM((2, rows, depth // n_dp), BF16),
            pltpu.VMEM((head, rows), BF16), pltpu.VMEM((head, rows), BF16),
            pltpu.VMEM((2, n_ctx, 128, 128), F32),
            pltpu.VMEM((nz, 2, 128, 128), BF16), pltpu.VMEM((nz, 2, 128, 128), BF16),
            pltpu.VMEM((n_ctx, 128, 128), BF16), pltpu.VMEM((n_ctx, 128, 128), BF16),
            pltpu.VMEM((nz, 128, 128), BF16), pltpu.VMEM((nz, 128, 128), BF16),
            pltpu.VMEM((n_ctx, 128, 128), BF16),
            dma((2,)), dma((2,)), dma((2,)), dma((1,)), dma((1,)), dma((nz,)), dma((nz,)), dma((n_ctx,)), dma((n_ctx,)),
            dma((nz,)), dma((nz,)), dma((2 * nz,)), dma((2 * nz,)),
        ]
    got = pl.pallas_call(
        functools.partial(kernel, n_ctx, n_dp, reduce_here),
        out_shape=out_shape,
        in_specs=[pl.BlockSpec(memory_space=pltpu.HBM)] * 8,
        out_specs=[any_space] * len(out_shape),
        scratch_shapes=scratch,
        compiler_params=pltpu.CompilerParams(
            collective_id=0, has_side_effects=True, vmem_limit_bytes=56 * 1024 * 1024
        ),
    )(query, keys, values, attn_out, out_grad, lse, doc_start, inputs)
    if reduce_here:
        return tuple(hand_over(got))
    dq, dk, dv = got
    term = lax.dot_general(
        inputs[0], dk[0], (((0,), (0,)), ((), ())), preferred_element_type=jnp.float32
    )
    return dq, dk, dv, lax.psum(lax.psum_scatter(term, "dp", scatter_dimension=0, tiled=True), "ctx")


def solution(mesh):
    in_specs = (
        P("dp", "ctx", None),
        P("dp", "ctx", None),
        P("dp", "ctx", None),
        P("dp", "ctx", None),
        P("dp", "ctx", None),
        P("dp", None, "ctx"),
        P("dp", "ctx"),
        P("dp", "ctx", None),
    )
    out_specs = (P("dp", "ctx", None), P("dp", "ctx", None), P("dp", "ctx", None), P("dp", None))
    return jax.shard_map(
        functools.partial(local, mesh.shape["ctx"], mesh.shape["dp"]),
        mesh=mesh, in_specs=in_specs, out_specs=out_specs, check_vma=False,
    )
```

```python
import functools

import jax
import jax.numpy as jnp
from jax import lax
from jax.experimental import pallas as pl
from jax.experimental.pallas import tpu as pltpu
from jax.sharding import PartitionSpec as P

QH = 8
WINDOW = 256
F32 = jnp.float32
BF16 = jnp.bfloat16
NT = (((1,), (1,)), ((), ()))


def dot(a, b):
    return jnp.dot(a, b, preferred_element_type=F32)


def dot_nt(a, b):
    return lax.dot_general(a, b, NT, preferred_element_type=F32)


def remote(src, dst, send, recv, where):
    return pltpu.make_async_remote_copy(
        src_ref=src, dst_ref=dst, send_sem=send, recv_sem=recv,
        device_id=where, device_id_type=pl.DeviceIdType.MESH,
    )


def kernel(n_ctx, n_dp, reduce_here, *refs):
    (q_in, k_in, v_in, o_in, g_in, lse_in, start_in, x_in) = refs[:8]
    n_out = 4 if reduce_here else 3
    outs = refs[8:8 + n_out]
    dq_out, dk_out, dv_out = outs[:3]
    scratch = refs[8 + n_out:]
    (q, k, v, o, g, lse, start, delta, kp, vp, ds_all, dq, dk_own, dv_own, dk_near, dv_near,
     dk_send, dv_send, dk_back, dv_back, dk_low, dv_low, load, store, halo_s, halo_r, back_s, back_r, probs) = scratch[:29]
    rows, width = q.shape
    head = width // QH
    scale = head ** (-0.5)
    c = lax.axis_index("ctx")
    d = lax.axis_index("dp")
    after = lax.rem(c + 1, n_ctx)
    before = lax.rem(c + n_ctx - 1, n_ctx)

    loads = [
        pltpu.make_async_copy(src.at[0], dst, load.at[i])
        for i, (src, dst) in enumerate(
            ((k_in, k), (v_in, v), (q_in, q), (g_in, g), (o_in, o), (lse_in, lse))
        )
    ]
    loads.append(pltpu.make_async_copy(start_in, start, load.at[6]))
    for copy in loads:
        copy.start()

    partners = [(after, d), (before, d)]
    if reduce_here:
        (tot_out,) = outs[3:]
        (xl, xr, dkt, dkt_r, wf, s1, r1, s2, r2, s3, r3, gb,
         xload, x_s, x_r, t_s, t_r, p1_s, p1_r, p2_s, p2_r, p3_s, p3_r, ag_s, ag_r) = scratch[29:]
        nz = n_ctx // 2
        block = x_in.shape[2] // n_dp
        core, y = lax.rem(d, 2), d // 2
        xx, z = lax.rem(c, 2), c // 2
        at_core = (c, y * 2 + 1 - core)
        at_y = (c, (1 - y) * 2 + core)
        far = [(s, e) for s in range(1, nz) for e in (0, 1)] + [(0, 1)]
        at = {(s, e): (lax.rem(z + s, nz) * 2 + (1 - xx if e else xx), d) for s, e in far}
        at_x = at[0, 1]
        partners += [at_core, at_y] + [at[one] for one in far]
    barrier = pltpu.get_barrier_semaphore()
    for where in partners:
        pl.semaphore_signal(barrier, inc=1, device_id=where, device_id_type=pl.DeviceIdType.MESH)
    pl.semaphore_wait(barrier, len(partners))

    halo = [
        remote(src.at[0], dst, halo_s.at[i], halo_r.at[i], (after, d))
        for i, (src, dst) in enumerate(((k_in, kp), (v_in, vp)))
    ]
    for copy in halo:
        copy.start()
    if reduce_here:
        xcopies = []
        for yy in range(2):
            mine = pl.ds(pl.multiple_of((yy * 2 + core) * block, block), block)
            other = pl.ds(pl.multiple_of((yy * 2 + 1 - core) * block, block), block)
            xcopies.append(pltpu.make_async_copy(x_in.at[0, :, mine], xl.at[yy], xload.at[yy]))
            xcopies.append(remote(x_in.at[0, :, other], xr.at[yy], x_s.at[yy], x_r.at[yy], at_core))
        for copy in xcopies:
            copy.start()

    for copy in loads:
        copy.wait()
    lane = lax.broadcasted_iota(jnp.int32, (rows, 128), 1)
    spread = jnp.zeros((rows, 128), F32)
    for h in range(QH):
        cols = slice(h * head, (h + 1) * head)
        one = jnp.sum(g[:, cols].astype(F32) * o[:, cols].astype(F32), axis=1, keepdims=True)
        spread = jnp.where(lane == h, one, spread)
    delta[...] = spread.T[:QH]

    s_at = lax.broadcasted_iota(jnp.int32, (rows, rows), 0)
    t_at = lax.broadcasted_iota(jnp.int32, (rows, rows), 1)
    first = start[...] - c * rows

    def part(keys, values, allowed, base, dk_sum, dv_sum):
        def one(h):
            cols = slice(h * head, (h + 1) * head)
            qh, gh = q[:, cols], g[:, cols]
            s = dot_nt(keys[...], qh)
            dp = dot_nt(values[...], gh)
            p = jnp.where(allowed, jnp.exp(s * scale - lse[h:h + 1, :]), 0.0)
            low = p.astype(BF16)
            sg = (p * (dp - delta[h:h + 1, :]) * scale).astype(BF16)
            ds_all[h, base:base + rows, :] = sg
            return dot(sg, qh), dot(low, gh)

        def body(i, carry):
            a, b = one(2 * i), one(2 * i + 1)
            dk_sum[...] += a[0] + b[0]
            dv_sum[...] += a[1] + b[1]
            return carry

        dk_sum[...] = jnp.zeros_like(dk_sum)
        dv_sum[...] = jnp.zeros_like(dv_sum)
        for i in range(QH // 2):
            body(i, 0)

    part(k, v, (s_at >= first) & (s_at <= t_at), 0, dk_own, dv_own)
    near = (s_at - WINDOW >= first) & (t_at - s_at + WINDOW < WINDOW)
    halo[0].wait()
    for h in range(QH):
        cols = slice(h * head, (h + 1) * head)
        score = dot_nt(kp[...], q[:, cols]) * scale - lse[h:h + 1, :]
        p = jnp.where(near, jnp.exp(score), 0.0)
        probs[h] = p
        term = dot(p.astype(BF16), g[:, cols])
        dv_near[...] = term if h == 0 else dv_near[...] + term
    halo[1].wait()
    for h in range(QH):
        cols = slice(h * head, (h + 1) * head)
        dp = dot_nt(vp[...], g[:, cols])
        sg = (probs[h] * (dp - delta[h:h + 1, :]) * scale).astype(BF16)
        ds_all[h, rows:, :] = sg
        term = dot(sg, q[:, cols])
        dk_near[...] = term if h == 0 else dk_near[...] + term
    dk_send[...] = dk_near[...].astype(BF16)
    back = [
        remote(src, dst, back_s.at[i], back_r.at[i], (before, d))
        for i, (src, dst) in enumerate(((dk_send, dk_back), (dv_send, dv_back)))
    ]
    back[0].start()
    dv_send[...] = dv_near[...].astype(BF16)
    back[1].start()

    kt = jnp.concatenate([k[...].astype(F32).T, kp[...].astype(F32).T], axis=1).astype(BF16)

    def dq_heads(lo, hi):
        for h in range(lo, hi):
            cols = slice(h * head, (h + 1) * head)
            dq[:, cols] = dot(kt, ds_all[h]).T.astype(BF16)

    def finish_dq():
        dq_heads(QH // 2, QH)
        copy = pltpu.make_async_copy(dq, dq_out.at[0], store.at[0])
        copy.start()
        return copy

    dq_heads(0, QH // 2)

    back[0].wait()
    dk = dk_own[...] + dk_back[...].astype(F32)
    dk_low[...] = dk.astype(BF16)
    dk_store = pltpu.make_async_copy(dk_low, dk_out.at[0], store.at[1])

    if reduce_here:
        dkt[...] = dk.T.astype(BF16)
        trade = remote(dkt, dkt_r, t_s.at[0], t_r.at[0], at_core)
        trade.start()
    dk_store.start()

    def finish_dv():
        back[1].wait()
        dv_low[...] = (dv_own[...] + dv_back[...].astype(F32)).astype(BF16)
        copy = pltpu.make_async_copy(dv_low, dv_out.at[0], store.at[2])
        copy.start()
        return copy

    if reduce_here:
        for copy in xcopies:
            copy.wait()
        steps = list(range(1, nz)) + [0]
        places = [lax.rem(z + s, nz) for s in range(nz)]

        def chunk(src, left, yy, s):
            cols = pl.ds(pl.multiple_of(places[s] * 256, 256), 256)
            return dot(left[...], src[yy, :, cols])

        for yy in (1 - y, y):
            for s in steps:
                got = chunk(xl, dkt, yy, s)
                wf[yy, 2 * s] = got[:, :128]
                wf[yy, 2 * s + 1] = got[:, 128:]
        trade.wait()

        def add(yy, s):
            got = chunk(xr, dkt_r, yy, s)
            wf[yy, 2 * s] += got[:, :128]
            wf[yy, 2 * s + 1] += got[:, 128:]

        first_out, second_out, out = {}, {}, {}
        for s in steps:
            add(1 - y, s)
            if s % 2:
                s1[s, 0] = wf[1 - y, 2 * s].astype(BF16)
                s1[s, 1] = wf[1 - y, 2 * s + 1].astype(BF16)
            else:
                add(y, s)
                s1[s, 0] = wf[0, 2 * s + 1 - xx].astype(BF16)
                s1[s, 1] = wf[1, 2 * s + 1 - xx].astype(BF16)
            first_out[s] = remote(
                s1.at[s], r1.at[s], p1_s.at[s], p1_r.at[s], at_y if s % 2 else at_x
            )
            first_out[s].start()
        for s in steps:
            if s % 2:
                add(y, s)

        def to_owner(s, e, piece):
            n = 2 * s + e
            s2[n] = piece.astype(BF16)
            out[s, e] = remote(s2.at[n], r2.at[n], p2_s.at[n], p2_r.at[n], at[s, e])
            out[s, e].start()

        for s in steps:
            first_out[s].wait_recv()
            if s % 2:
                for e in (0, 1):
                    half = 1 - xx if e else xx
                    to_owner(s, e, wf[y, 2 * s + half] + r1[s, half].astype(F32))
            else:
                s3[s] = (wf[1 - y, 2 * s + xx] + r1[s, 1 - y].astype(F32)).astype(BF16)
                second_out[s] = remote(s3.at[s], r3.at[s], p3_s.at[s], p3_r.at[s], at_y)
                second_out[s].start()
        for s in steps:
            if s % 2 == 0:
                second_out[s].wait_recv()
                piece = wf[y, 2 * s + xx] + r1[s, y].astype(F32) + r3[s].astype(F32)
                if s:
                    to_owner(s, 0, piece)
                else:
                    total = piece
        dv_store = finish_dv()
        dq_store = finish_dq()
        for s, e in out:
            out[s, e].wait_recv()
            total = total + r2[2 * s + e].astype(F32)
        gb[c] = total.T.astype(BF16)

        over_z = [
            remote(gb.at[c], gb.at[c], ag_s.at[s], ag_r.at[s], at[s, 0]) for s in range(1, nz)
        ]
        over_x = [remote(gb.at[c], gb.at[c], ag_s.at[nz], ag_r.at[nz], at_x)]
        for copy in over_z + over_x:
            copy.start()
        kept = []

        def keep(slot, n):
            kept.append(pltpu.make_async_copy(gb.at[slot], tot_out.at[slot], store.at[n]))
            kept[-1].start()

        keep(c, 3)
        for s in range(1, nz):
            over_z[s - 1].wait_recv()
            slot = lax.rem(z - s + nz, nz) * 2 + xx
            copy = remote(gb.at[slot], gb.at[slot], ag_s.at[nz + s], ag_r.at[nz + s], at_x)
            copy.start()
            over_x.append(copy)
            keep(slot, 3 + s)
        for s in range(nz):
            over_x[s].wait_recv()
            keep(lax.rem(z - s + nz, nz) * 2 + 1 - xx, 3 + nz + s)
        for copy in [*first_out.values(), *second_out.values(), *out.values()] + over_z + over_x:
            copy.wait_send()
        for copy in kept:
            copy.wait()
    else:
        dv_store = finish_dv()
        dq_store = finish_dq()
    dq_store.wait()
    dk_store.wait()
    dv_store.wait()


def hand_over_kernel(count, *refs):
    arrays, outs, held = refs[:count], refs[count:2 * count], refs[2 * count:3 * count]
    wide, arrive, leave = refs[3 * count:]
    loads = [pltpu.make_async_copy(arrays[i], held[i], arrive.at[i]) for i in range(count)]
    stores = [pltpu.make_async_copy(held[i], outs[i], leave.at[i]) for i in range(count - 1)]
    stores.append(pltpu.make_async_copy(wide, outs[-1], leave.at[count - 1]))
    places = [count - 1] + list(range(count - 1))
    for i in places:
        loads[i].start()
    for i in places:
        loads[i].wait()
        if i == count - 1:
            wide[...] = held[i][...].astype(F32).reshape(wide.shape)
        stores[i].start()
    for copy in stores:
        copy.wait()


def hand_over(arrays):
    *same, last = arrays
    count = len(arrays)
    total = jax.ShapeDtypeStruct((last.shape[0] * last.shape[1], last.shape[2]), F32)
    return pl.pallas_call(
        functools.partial(hand_over_kernel, count),
        out_shape=[jax.ShapeDtypeStruct(a.shape, a.dtype) for a in same] + [total],
        in_specs=[pl.BlockSpec(memory_space=pl.ANY)] * count,
        out_specs=[pl.BlockSpec(memory_space=pltpu.HBM)] * count,
        scratch_shapes=[pltpu.VMEM(a.shape, a.dtype) for a in arrays]
        + [pltpu.VMEM(total.shape, F32), pltpu.SemaphoreType.DMA((count,)), pltpu.SemaphoreType.DMA((count,))],
    )(*arrays)


def local(n_ctx, n_dp, query, keys, values, attn_out, out_grad, lse, doc_start, inputs):
    _, rows, width = query.shape
    head = width // QH
    depth = inputs.shape[2]
    reduce_here = n_dp == 4 and n_ctx % 4 == 0 and rows == WINDOW and depth == n_dp * n_ctx * 128 and head == 128
    nz = n_ctx // 2
    any_space = pl.BlockSpec(memory_space=pl.ANY)
    out_shape = [
        jax.ShapeDtypeStruct(query.shape, BF16),
        jax.ShapeDtypeStruct(keys.shape, BF16),
        jax.ShapeDtypeStruct(keys.shape, BF16),
    ]
    dma = pltpu.SemaphoreType.DMA
    small = pltpu.VMEM((rows, head), BF16)
    wide = pltpu.VMEM((rows, head), F32)
    full = pltpu.VMEM((rows, width), BF16)
    scratch = [
        full, small, small, full, full, pltpu.VMEM((QH, rows), F32), pltpu.VMEM((1, rows), jnp.int32),
        pltpu.VMEM((QH, rows), F32), small, small, pltpu.VMEM((QH, 2 * rows, rows), BF16), full,
        wide, wide, wide, wide, small, small, small, small, small, small,
        dma((7,)), dma((3 + n_ctx,)), dma((2,)), dma((2,)), dma((2,)), dma((2,)),
        pltpu.VMEM((QH, rows, rows), F32),
    ]
    if reduce_here:
        out_shape.append(jax.ShapeDtypeStruct((n_ctx, 128, head), BF16))
        scratch += [
            pltpu.VMEM((2, rows, depth // n_dp), BF16), pltpu.VMEM((2, rows, depth // n_dp), BF16),
            pltpu.VMEM((head, rows), BF16), pltpu.VMEM((head, rows), BF16),
            pltpu.VMEM((2, n_ctx, 128, 128), F32),
            pltpu.VMEM((nz, 2, 128, 128), BF16), pltpu.VMEM((nz, 2, 128, 128), BF16),
            pltpu.VMEM((n_ctx, 128, 128), BF16), pltpu.VMEM((n_ctx, 128, 128), BF16),
            pltpu.VMEM((nz, 128, 128), BF16), pltpu.VMEM((nz, 128, 128), BF16),
            pltpu.VMEM((n_ctx, 128, 128), BF16),
            dma((2,)), dma((2,)), dma((2,)), dma((1,)), dma((1,)), dma((nz,)), dma((nz,)), dma((n_ctx,)), dma((n_ctx,)),
            dma((nz,)), dma((nz,)), dma((2 * nz,)), dma((2 * nz,)),
        ]
    got = pl.pallas_call(
        functools.partial(kernel, n_ctx, n_dp, reduce_here),
        out_shape=out_shape,
        in_specs=[pl.BlockSpec(memory_space=pltpu.HBM)] * 8,
        out_specs=[any_space] * len(out_shape),
        scratch_shapes=scratch,
        compiler_params=pltpu.CompilerParams(
            collective_id=0, has_side_effects=True, vmem_limit_bytes=56 * 1024 * 1024
        ),
    )(query, keys, values, attn_out, out_grad, lse, doc_start, inputs)
    if reduce_here:
        return tuple(hand_over(got))
    dq, dk, dv = got
    term = lax.dot_general(
        inputs[0], dk[0], (((0,), (0,)), ((), ())), preferred_element_type=jnp.float32
    )
    return dq, dk, dv, lax.psum(lax.psum_scatter(term, "dp", scatter_dimension=0, tiled=True), "ctx")


def solution(mesh):
    in_specs = (
        P("dp", "ctx", None),
        P("dp", "ctx", None),
        P("dp", "ctx", None),
        P("dp", "ctx", None),
        P("dp", "ctx", None),
        P("dp", None, "ctx"),
        P("dp", "ctx"),
        P("dp", "ctx", None),
    )
    out_specs = (P("dp", "ctx", None), P("dp", "ctx", None), P("dp", "ctx", None), P("dp", None))
    return jax.shard_map(
        functools.partial(local, mesh.shape["ctx"], mesh.shape["dp"]),
        mesh=mesh, in_specs=in_specs, out_specs=out_specs, check_vma=False,
    )
```
